32 devices in a mesh: segment: 4 (over z), dp: 2 (over x), tensor: 4 (over y, core).
Axes of the slice: x: 2, y: 2, z: 4, core: 2. Of those that a mesh axis runs over, the one named last changes fastest.
Arguments:
- inbound: bfloat16 [4, 2, 512, 4096], P('segment', None, 'dp'), may hold values from -21 to 21
- weights: bfloat16 [4, 4096, 3, 4096], P('segment', None, None, 'tensor'), may hold values from -0.09375 to 0.09375
- cotangent: bfloat16 [4, 2, 512, 4096], P('segment', None, 'dp', 'tensor'), may hold values from -20 to 20
Outputs:
- section_out: bfloat16 [4, 2, 512, 4096], P('segment', None, 'dp', 'tensor')
The draws below stay inside these ranges and needn't reach their ends.
All inputs are finite; a program needn't handle non-finite values.
Results may differ from the reference program's by a relative error of at most 0.022.
The reference program's roundings to bfloat16 on the way count: a program that leaves them out, or rounds other values in their place, can miss the bound.
Values may be sent and summed in bfloat16 or wider, within the bound.
A program may use at most 128 MiB of HBM per device.

```python
import math
import jax
import jax.numpy as jnp
from jax import lax

D = 4096
HD = 64
HEADS = 64
MB = 2
TOK = 512
N_SEGMENT = 4
N_TENSOR = 4


def draw_inbound(key, part):
    first_key, second_key = jax.random.split(key)
    base = jnp.clip(jax.random.normal(first_key, (N_SEGMENT, MB, TOK, D), jnp.float32), -6.0, 6.0)
    row_scale = jnp.exp(jax.random.uniform(second_key, (N_SEGMENT, MB, TOK, 1), jnp.float32, math.log(0.5), math.log(2.0)))
    return (base * row_scale).astype(jnp.bfloat16)


def draw_cotangent(key, part):
    slot_scale = jnp.where(jnp.arange(N_SEGMENT) == 0, 0.3, 4.0).astype(jnp.float32)[:, None, None, None]
    base = jnp.clip(jax.random.normal(key, (N_SEGMENT, MB, TOK, D), jnp.float32), -5.0, 5.0)
    return (base * slot_scale).astype(jnp.bfloat16)


def shard_levels(own_key, extent, cuts, least, high):
    level = 1.0
    for position, shards_of in cuts:
        draws = jax.random.uniform(jax.random.fold_in(jax.random.fold_in(own_key, 6), position), (shards_of,), jnp.float32, least / len(cuts), high / len(cuts))
        level = level * jnp.repeat(jnp.exp(draws), extent[position] // shards_of).reshape((-1,) + (1,) * (len(extent) - 1 - position))
    return level


def normal_values(key, dims, deviation, limit, cuts=(), kind=jnp.bfloat16):
    drawn = deviation * jax.random.normal(key, dims, jnp.float32)
    if cuts:
        drawn = drawn * shard_levels(key, dims, cuts, -0.22, 0.18)
    return jnp.clip(drawn, -limit, limit).astype(kind)


def setup_inputs(seed: int = 0) -> dict:
    keys = jax.random.split(jax.random.key(seed), 4)
    inbound = draw_inbound(jax.random.fold_in(keys[3], 71), 0)
    weights = normal_values(keys[1], (N_SEGMENT, D, 3, D), D ** -0.5, 0.09375, ((0, 4), (3, 4)))
    cotangent = draw_cotangent(jax.random.fold_in(keys[3], 71), 0)
    return {"inbound": inbound, "weights": weights, "cotangent": cotangent}


def one_section(section_states, encoder_states, section_weights, upstream):
    row_total = MB * TOK
    feat_width = D // N_TENSOR
    score_scale = HD ** -0.5
    query = jnp.dot(section_states.reshape(row_total, D), section_weights[:, 0, :], preferred_element_type=jnp.float32).astype(jnp.bfloat16)
    flat_enc = encoder_states.reshape(row_total, D)
    key_rows = jnp.dot(flat_enc, section_weights[:, 1, :], preferred_element_type=jnp.float32).astype(jnp.bfloat16)
    value_rows = jnp.dot(flat_enc, section_weights[:, 2, :], preferred_element_type=jnp.float32).astype(jnp.bfloat16)
    query_heads = query.reshape(MB, TOK, HEADS, HD).astype(jnp.float32)
    key_heads = key_rows.reshape(MB, TOK, HEADS, HD).astype(jnp.float32)
    value_heads = value_rows.reshape(MB, TOK, HEADS, HD).astype(jnp.float32)
    scores = jnp.einsum("mqhe,mkhe->mhqk", query_heads, key_heads) * score_scale
    score_peak = jnp.max(scores, axis=-1, keepdims=True)
    exp_scores = jnp.exp(scores - score_peak)
    attend_prob = exp_scores / jnp.sum(exp_scores, axis=-1, keepdims=True)
    prob_rounded = attend_prob.astype(jnp.bfloat16).astype(jnp.float32)
    context = jnp.einsum("mhqk,mkhe->mqhe", prob_rounded, value_heads).astype(jnp.bfloat16).reshape(MB, TOK, D)
    grad_heads = upstream.reshape(MB, TOK, HEADS, HD).astype(jnp.float32)
    prob_grad = jnp.einsum("mqhe,mkhe->mhqk", grad_heads, value_heads)
    row_delta = jnp.sum(attend_prob * prob_grad, axis=-1, keepdims=True)
    score_grad = (attend_prob * (prob_grad - row_delta) * score_scale).astype(jnp.bfloat16).astype(jnp.float32)
    key_grad = jnp.einsum("mhqk,mqhe->mkhe", score_grad, query_heads).astype(jnp.bfloat16)
    value_grad = jnp.einsum("mhqk,mqhe->mkhe", prob_rounded, grad_heads).astype(jnp.bfloat16)
    joined_grads = jnp.concatenate([key_grad.reshape(row_total, N_TENSOR, feat_width), value_grad.reshape(row_total, N_TENSOR, feat_width)], axis=2)
    joined_weights = jnp.concatenate([section_weights[:, 1, :].reshape(D, N_TENSOR, feat_width), section_weights[:, 2, :].reshape(D, N_TENSOR, feat_width)], axis=2)
    group_terms = jnp.einsum("rtc,dtc->trd", joined_grads.astype(jnp.float32), joined_weights.astype(jnp.float32))
    rounded_terms = lax.optimization_barrier(group_terms.astype(jnp.bfloat16)).astype(jnp.float32)
    section_grad = jnp.sum(rounded_terms, axis=0).reshape(MB, TOK, D)
    return context, section_grad


def reference(inbound, weights, cotangent):
    encoder_states = inbound[0]

    def run_section(index):
        return one_section(inbound[index], encoder_states, weights[index], cotangent[index])

    contexts, section_grads = lax.map(run_section, jnp.arange(1, N_SEGMENT, dtype=jnp.int32))
    encoder_grad = (cotangent[0].astype(jnp.float32) + jnp.sum(section_grads, axis=0)).astype(jnp.bfloat16)
    return jnp.concatenate([encoder_grad[None], contexts], axis=0)
```

```python
import jax
import jax.numpy as jnp
from jax import lax
from jax.experimental import pallas as pl
from jax.experimental.pallas import tpu as pltpu
from jax.sharding import PartitionSpec as P

HD = 64


def broadcast(value, axis, root):
    mine = lax.axis_index(axis) == root
    return lax.psum(jnp.where(mine, value, jnp.zeros_like(value)), axis)


def shards(inbound, weights, cotangent):
    states = inbound[0]
    micro_count, row_count, model_width = states.shape
    encoded = broadcast(states, "segment", 0)
    section_layer = weights[0]
    feat_width = section_layer.shape[2]
    head_count = feat_width // HD
    score_scale = HD ** (-0.5)
    query = jnp.dot(
        states.reshape(micro_count * row_count, model_width),
        section_layer[:, 0, :],
        preferred_element_type=jnp.float32,
    ).astype(jnp.bfloat16)
    query = query.reshape(micro_count, row_count, feat_width)
    upstream = cotangent[0]
    pair_weights = section_layer[:, 1:, :].reshape(model_width, 2 * feat_width)
    keyval = jnp.dot(
        encoded.reshape(micro_count * row_count, model_width),
        pair_weights,
        preferred_element_type=jnp.float32,
    ).astype(jnp.bfloat16)
    keyval = keyval.reshape(micro_count, row_count, 2, feat_width)
    all_keyval = lax.all_gather(keyval, "dp", axis=1, tiled=True)
    key_count = all_keyval.shape[1]
    all_query, all_upstream = (query, upstream)
    query_count = all_query.shape[1]

    def attend(items):
        query_one, upstream_one, keyval_one = items
        query_heads = query_one.reshape(query_count, head_count, HD)
        grad_heads = upstream_one.reshape(query_count, head_count, HD)
        key_heads = keyval_one[:, 0].reshape(key_count, head_count, HD)
        value_heads = keyval_one[:, 1].reshape(key_count, head_count, HD)
        scores = (
            jnp.einsum("qhe,khe->hqk", query_heads, key_heads, preferred_element_type=jnp.float32)
            * score_scale
        )
        score_peak = jnp.max(scores, axis=-1, keepdims=True)
        exp_scores = jnp.exp(scores - score_peak)
        attend_prob = exp_scores / jnp.sum(exp_scores, axis=-1, keepdims=True)
        prob_rounded = attend_prob.astype(jnp.bfloat16)
        prob_grad = jnp.einsum(
            "qhe,khe->hqk", grad_heads, value_heads, preferred_element_type=jnp.float32
        )
        row_delta = jnp.sum(attend_prob * prob_grad, axis=-1, keepdims=True)
        score_grad = (attend_prob * (prob_grad - row_delta) * score_scale).astype(jnp.bfloat16)
        context = jnp.einsum(
            "hqk,khe->qhe", prob_rounded, value_heads, preferred_element_type=jnp.float32
        )
        key_grad = jnp.einsum(
            "hqk,qhe->khe", score_grad, query_heads, preferred_element_type=jnp.float32
        )
        value_grad = jnp.einsum(
            "hqk,qhe->khe", prob_rounded, grad_heads, preferred_element_type=jnp.float32
        )
        context = context.astype(jnp.bfloat16).reshape(row_count, feat_width)
        joined = jnp.stack(
            [key_grad.reshape(-1, feat_width), value_grad.reshape(-1, feat_width)], axis=1
        )
        return (context, joined)

    context, joined_grads = lax.map(attend, (all_query, all_upstream, all_keyval))
    owned_grads = lax.psum_scatter(joined_grads, "dp", scatter_dimension=1, tiled=True).astype(
        jnp.bfloat16
    )
    head_terms = jnp.einsum(
        "rc,dc->rd",
        owned_grads.reshape(micro_count * row_count, 2 * feat_width),
        pair_weights,
        preferred_element_type=jnp.float32,
    )
    head_terms = head_terms.reshape(micro_count, row_count, model_width)
    heads_total = lax.psum_scatter(
        head_terms.astype(jnp.bfloat16), "tensor", scatter_dimension=2, tiled=True
    ).astype(jnp.float32)
    segment_index = lax.axis_index("segment")
    live_mask = (segment_index > 0).astype(jnp.float32)
    sections = lax.psum(heads_total * live_mask, "segment")
    encoder_grad = (sections + cotangent[0].astype(jnp.float32)).astype(jnp.bfloat16)
    result = jnp.where(segment_index == 0, encoder_grad, context)
    return result[None]


CHUNKS = 4


def relay_kernel(n_segment, x_ref, w_ref, g_ref, out_ref,
                 enc, own_x, wq, wkv, cot0, parts, ctx, rctx, dkv, rdkv,
                 core_out, core_in, y_out, y_in, total, z_out, z_in,
                 load_x, load_w, load_q, load_g,
                 zs, zr, cs, cr, ys, yr, fs, fr, xs, xr, ds_, dr, ts, tr,
                 ks, kr, vs, vr, us, ur):
    micro, rows, width = x_ref.shape
    feat = w_ref.shape[2]
    half = feat // 2
    quarter = half // 2
    piece = rows // 4
    crow = piece // CHUNKS
    steps = micro * CHUNKS
    zrow = rows // CHUNKS
    pairs = half // 128

    seg = lax.axis_index("segment")
    d = lax.axis_index("dp")
    t = lax.axis_index("tensor")
    y, c = t // 2, t % 2
    peer_x = {"dp": 1 - d}
    peer_c = {"tensor": y * 2 + (1 - c)}
    peer_y = {"tensor": (1 - y) * 2 + c}
    up = {"segment": lax.min(seg + 1, n_segment - 1)}
    down = {"segment": lax.max(seg - 1, 0)}
    first, last = seg == 0, seg == n_segment - 1
    MESH = pl.DeviceIdType.MESH

    def remote(src, dst, s, r, dev):
        return pltpu.make_async_remote_copy(
            src_ref=src, dst_ref=dst, send_sem=s, recv_sem=r,
            device_id=dev, device_id_type=MESH)

    def slot(ref, who, j):
        row = pl.multiple_of(who * piece + lax.rem(j, CHUNKS) * crow, crow)
        return ref.at[j // CHUNKS, pl.ds(row, crow), :]

    def z_copy(ref, j):
        return remote(slot(ref, t, j), slot(enc, t, j), zs.at[j], zr.at[j], up)

    def c_copy(j):
        return remote(slot(enc, t, j), slot(enc, t, j), cs.at[j], cr.at[j], peer_c)

    def y_copy(j):
        return remote(slot(enc, t, j), slot(enc, t, j), ys.at[j], yr.at[j], peer_y)

    ty = (1 - y) * 2 + c

    def f_copy(j):
        return remote(slot(enc, ty, j), slot(enc, ty, j), fs.at[j], fr.at[j], peer_c)

    def lanes(which, size):
        return pl.ds(pl.multiple_of(which * size, size), size)

    def x_copy(kind, m):
        i = kind * micro + m
        return remote(parts.at[kind, m, 2], parts.at[kind, m, d], xs.at[i], xr.at[i], peer_x)

    def g_copy(m):
        i = 3 * micro + m
        return remote(g_ref.at[m, :, lanes(1 - d, half)], parts.at[3, m, d],
                      xs.at[i], xr.at[i], peer_x)

    def g_load(m):
        return pltpu.make_async_copy(g_ref.at[m, :, lanes(d, half)], parts.at[3, m, d], load_g.at[m])

    def q_load(n):
        h = jnp.where(n < 2, 1 - d, d)
        col = pl.multiple_of(h * half + lax.rem(n, 2) * quarter, quarter)
        b = lax.rem(n, 2)
        return pltpu.make_async_copy(w_ref.at[0, :, pl.ds(col, quarter)], wq.at[b], load_q.at[b])

    def w_load(k):
        return pltpu.make_async_copy(w_ref.at[k + 1], wkv.at[k], load_w.at[k])

    def d_copy(m, p):
        i = m * pairs + p
        lane = lanes(p, 128)
        return remote(dkv.at[m, 1 - d, :, :, lane], rdkv.at[m, :, :, lane], ds_.at[i], dr.at[i], peer_x)

    def t_copy(m, p):
        i = m * pairs + p
        lane = lanes(p, 128)
        return remote(ctx.at[m, 1 - d, :, lane], rctx.at[m, :, lane], ts.at[i], tr.at[i], peer_x)

    def k_copy(m, yy):
        i = m * 2 + yy
        return remote(core_out.at[m, yy], core_in.at[m, yy], ks.at[i], kr.at[i], peer_c)

    def v_copy(i):
        m, row = i // CHUNKS, pl.multiple_of(lax.rem(i, CHUNKS) * zrow, zrow)
        return remote(y_out.at[m, pl.ds(row, zrow), :], y_in.at[m, pl.ds(row, zrow), :],
                      vs.at[i], vr.at[i], peer_y)

    def u_copy(i):
        m, row = i // CHUNKS, pl.multiple_of(lax.rem(i, CHUNKS) * zrow, zrow)
        return remote(z_out.at[m, pl.ds(row, zrow), :], z_in.at[m, pl.ds(row, zrow), :],
                      us.at[i], ur.at[i], down)

    x_load = pltpu.make_async_copy(x_ref, own_x, load_x)
    c_load = pltpu.make_async_copy(g_ref, cot0, load_x)

    barrier = pltpu.get_barrier_semaphore()
    for dev in (peer_x, peer_c, peer_y):
        pl.semaphore_signal(barrier, inc=1, device_id=dev, device_id_type=MESH)

    @pl.when(jnp.logical_not(last))
    def _():
        pl.semaphore_signal(barrier, inc=1, device_id=up, device_id_type=MESH)

    @pl.when(jnp.logical_not(first))
    def _():
        pl.semaphore_signal(barrier, inc=1, device_id=down, device_id_type=MESH)

    ends = first.astype(jnp.int32) + last.astype(jnp.int32)
    pl.semaphore_wait(barrier, 5 - ends)

    @pl.when(first)
    def _():
        def send(j, carry):
            z_copy(x_ref, j).start()
            return carry
        lax.fori_loop(0, steps, send, 0)
        c_load.start()
        c_load.wait()

        def finish(i, carry):
            u_copy(i).wait_recv()
            m, row = i // CHUNKS, pl.multiple_of(lax.rem(i, CHUNKS) * zrow, zrow)
            rr = pl.ds(row, zrow)
            out_ref[m, rr, :] = (z_in[m, rr, :].astype(jnp.float32)
                                 + cot0[m, rr, :].astype(jnp.float32)).astype(out_ref.dtype)
            return carry
        lax.fori_loop(0, steps, finish, 0)

        def drain(j, carry):
            z_copy(x_ref, j).wait_send()
            return carry
        lax.fori_loop(0, steps, drain, 0)

    @pl.when(jnp.logical_not(first))
    def _():
        x_load.start()
        q_load(0).start()
        q_load(1).start()
        for k in range(2):
            w_load(k).start()
        for m in range(micro):
            g_load(m).start()
            g_copy(m).start()

        def forward(j):
            z_copy(enc, j).wait_recv()

            @pl.when(jnp.logical_not(last))
            def _():
                z_copy(enc, j).start()
            y_copy(j).start()
            c_copy(j).start()

        def relay(j):
            y_copy(j).wait_recv()
            f_copy(j).start()

        x_load.wait()

        def q_step(j, carry):
            q_load(j).wait()
            value = jnp.dot(own_x[...].reshape(micro * rows, width), wq[lax.rem(j, 2)],
                            preferred_element_type=jnp.float32)
            value = (value * HD ** -0.5).astype(jnp.bfloat16).reshape(micro, rows, quarter)
            where = jnp.where(j < 2, 2, d)
            for m in range(micro):
                parts[0, m, where, :, lanes(lax.rem(j, 2), quarter)] = value[m]

            @pl.when(j < 2)
            def _():
                q_load(j + 2).start()

            @pl.when(j == 1)
            def _():
                for m in range(micro):
                    x_copy(0, m).start()
            forward(j)

            @pl.when(j > 0)
            def _():
                relay(j - 1)
            return carry
        lax.fori_loop(0, CHUNKS, q_step, 0)
        for k in range(2):
            w_load(k).wait()

        def gathered(m):
            def one(j, carry):
                c_copy(j).wait_recv()
                f_copy(j).wait_recv()
                return carry
            lax.fori_loop(m * CHUNKS, (m + 1) * CHUNKS, one, 0)

        def kv_step(i, carry):
            m, o = i // 4, lax.rem(i, 4)

            @pl.when(m == 0)
            def _():
                forward(CHUNKS + i)
                relay(CHUNKS + i - 1)

            @pl.when(i == 0)
            def _():
                gathered(0)

            @pl.when(i == 4)
            def _():
                relay(steps - 1)
                gathered(1)
            k = lax.rem(o, 2)
            h = jnp.where(o < 2, 1 - d, d)
            value = jnp.dot(enc[m], wkv[k, :, lanes(h, half)], preferred_element_type=jnp.float32)
            parts[1 + k, m, jnp.where(o < 2, 2, d)] = value.astype(jnp.bfloat16)

            @pl.when(o < 2)
            def _():
                x_copy(1 + k, m).start()
            return carry
        lax.fori_loop(0, 4 * micro, kv_step, 0)

        lane_id = lax.broadcasted_iota(jnp.int32, (1, 128), 1)
        f32 = jnp.float32

        def attend(m, lo, hi):
            def pair(p, carry):
                lane = lanes(p, 128)
                key = parts[1, m, 0:2, :, lane].reshape(2 * rows, 128)
                val = parts[2, m, 0:2, :, lane].reshape(2 * rows, 128)
                dk = jnp.zeros((2 * rows, 128), f32)
                dv = jnp.zeros((2 * rows, 128), f32)
                masks = [(lane_id < HD), (lane_id >= HD)]
                zero = jnp.zeros((), jnp.bfloat16)
                for b in range(2):
                    qry = parts[0, m, b, :, lane]
                    ups = parts[3, m, b, :, lane]
                    acc = jnp.zeros((128, rows), f32)
                    for mask in masks:
                        km = jnp.where(mask, key, zero)
                        vm = jnp.where(mask, val, zero)
                        nt = (((1,), (1,)), ((), ()))
                        sc = lax.dot_general(km, qry, nt, preferred_element_type=f32)
                        dp = lax.dot_general(vm, ups, nt, preferred_element_type=f32)
                        ex = jnp.exp(sc - jnp.max(sc, axis=0, keepdims=True))
                        pr = ex * (1.0 / jnp.sum(ex, axis=0, keepdims=True))
                        pb = pr.astype(jnp.bfloat16)
                        delta = jnp.sum(pr * dp, axis=0, keepdims=True)
                        sg = (pr * (dp - delta)).astype(jnp.bfloat16)
                        acc = acc + lax.dot_general(vm, pb, (((0,), (0,)), ((), ())),
                                                    preferred_element_type=f32)
                        dv = dv + jnp.dot(pb, jnp.where(mask, ups, zero), preferred_element_type=f32)
                        dk = dk + jnp.dot(sg, jnp.where(mask, qry, zero), preferred_element_type=f32)
                    ctx[m, b, :, lane] = acc.T.astype(jnp.bfloat16)
                dkb = dk.astype(jnp.bfloat16).reshape(2, rows, 128)
                dvb = dv.astype(jnp.bfloat16).reshape(2, rows, 128)
                for b in range(2):
                    dkv[m, b, 0, :, lane] = dkb[b]
                    dkv[m, b, 1, :, lane] = dvb[b]
                d_copy(m, p).start()
                t_copy(m, p).start()
                return carry
            lax.fori_loop(lo, hi, pair, 0)

        def term(m, col):
            value = None
            for h, ref in ((d, dkv.at[m, d]), (1 - d, rdkv.at[m])):
                for k in range(2):
                    part = lax.dot_general(
                        ref[k], wkv[k, pl.ds(pl.multiple_of(col, half), half), lanes(h, half)],
                        (((1,), (1,)), ((), ())), preferred_element_type=f32)
                    value = part if value is None else value + part
            return value

        def grads_out(m):
            def got(p, carry):
                d_copy(m, p).wait_recv()
                return carry
            lax.fori_loop(0, pairs, got, 0)

            def tile(k, carry):
                yy, o = k // 2, lax.rem(k, 2)
                col = (yy * 2 + 1 - c) * feat + o * half
                core_out[m, yy, :, lanes(o, half)] = term(m, col).astype(jnp.bfloat16)

                @pl.when(o == 1)
                def _():
                    k_copy(m, yy).start()
                return carry
            lax.fori_loop(0, 4, tile, 0)

        def grads_in(m):
            def tile(k, carry):
                o = lax.rem(k, 2)
                yy = jnp.where(k < 2, 1 - y, y)

                @pl.when(o == 0)
                def _():
                    k_copy(m, yy).wait_recv()
                col = (yy * 2 + c) * feat + o * half
                value = term(m, col) + core_in[m, yy, :, lanes(o, half)].astype(f32)

                @pl.when(k < 2)
                def _():
                    y_out[m, :, lanes(o, half)] = value.astype(jnp.bfloat16)

                @pl.when(k >= 2)
                def _():
                    total[m, :, lanes(o, half)] = value

                @pl.when(k == 1)
                def _():
                    for q in range(CHUNKS):
                        v_copy(m * CHUNKS + q).start()
                return carry
            lax.fori_loop(0, 4, tile, 0)

        def got_parts(m):
            for kind in range(3):
                x_copy(kind, m).wait_recv()
            g_copy(m).wait_recv()
            g_load(m).wait()

        got_parts(0)
        attend(0, 0, pairs)
        got_parts(1)
        attend(1, 0, pairs // 2)
        grads_out(0)
        attend(1, pairs // 2, pairs)
        grads_in(0)
        grads_out(1)
        grads_in(1)

        def chain(i, carry):
            m, row = i // CHUNKS, pl.multiple_of(lax.rem(i, CHUNKS) * zrow, zrow)
            rr = pl.ds(row, zrow)
            v_copy(i).wait_recv()
            total[m, rr, :] = total[m, rr, :] + y_in[m, rr, :].astype(f32)

            @pl.when(jnp.logical_not(last))
            def _():
                u_copy(i).wait_recv()
                total[m, rr, :] = total[m, rr, :] + z_in[m, rr, :].astype(f32)
            z_out[m, rr, :] = total[m, rr, :].astype(jnp.bfloat16)
            u_copy(i).start()
            return carry
        lax.fori_loop(0, steps, chain, 0)

        def context(i, carry):
            t_copy(i // pairs, lax.rem(i, pairs)).wait_recv()
            return carry
        lax.fori_loop(0, micro * pairs, context, 0)
        for m in range(micro):
            out_ref[m, :, lanes(d, half)] = ctx[m, d]
            out_ref[m, :, lanes(1 - d, half)] = rctx[m]

        def drain(i, carry):
            @pl.when(jnp.logical_not(last))
            def _():
                z_copy(enc, i).wait_send()
            c_copy(i).wait_send()
            y_copy(i).wait_send()
            f_copy(i).wait_send()
            v_copy(i).wait_send()
            u_copy(i).wait_send()
            return carry
        lax.fori_loop(0, steps, drain, 0)

        def drain_pairs(i, carry):
            d_copy(i // pairs, lax.rem(i, pairs)).wait_send()
            t_copy(i // pairs, lax.rem(i, pairs)).wait_send()
            return carry
        lax.fori_loop(0, micro * pairs, drain_pairs, 0)
        for m in range(micro):
            for kind in range(3):
                x_copy(kind, m).wait_send()
            g_copy(m).wait_send()
            for yy in range(2):
                k_copy(m, yy).wait_send()


def fused_shards(n_segment, inbound, weights, cotangent):
    micro, rows, width = inbound.shape[1:]
    feat = weights.shape[3]
    half = feat // 2
    steps, pairs = micro * CHUNKS, half // 128
    bf, f32 = jnp.bfloat16, jnp.float32
    vm, dma = pltpu.VMEM, pltpu.SemaphoreType.DMA
    scratch = [
        vm((micro, rows, width), bf),
        vm((micro, rows, width), bf),
        vm((2, width, half // 2), bf),
        vm((2, width, feat), bf),
        vm((micro, rows, feat), bf),
        vm((4, micro, 3, rows, half), bf),
        vm((micro, 2, rows, half), bf),
        vm((micro, rows, half), bf),
        vm((micro, 2, 2, rows, half), bf),
        vm((micro, 2, rows, half), bf),
        vm((micro, 2, rows, feat), bf),
        vm((micro, 2, rows, feat), bf),
        vm((micro, rows, feat), bf),
        vm((micro, rows, feat), bf),
        vm((micro, rows, feat), f32),
        vm((micro, rows, feat), bf),
        vm((micro, rows, feat), bf),
        dma, dma((2,)), dma((2,)), dma((micro,)),
    ]
    scratch += [dma((steps,))] * 8
    scratch += [dma((4 * micro,))] * 2
    scratch += [dma((micro * pairs,))] * 4
    scratch += [dma((2 * micro,))] * 2
    scratch += [dma((steps,))] * 4
    work = 2 * micro * rows * width * feat * 5
    out = pl.pallas_call(
        lambda *refs: relay_kernel(n_segment, *refs),
        out_shape=jax.ShapeDtypeStruct((micro, rows, feat), bf),
        in_specs=[pl.BlockSpec(memory_space=pl.ANY)] * 3,
        out_specs=pl.BlockSpec(memory_space=pltpu.VMEM),
        scratch_shapes=scratch,
        compiler_params=pltpu.CompilerParams(
            collective_id=0, has_side_effects=True, vmem_limit_bytes=62 * 1024 * 1024),
        cost_estimate=pl.CostEstimate(flops=work, bytes_accessed=32 << 20, transcendentals=1 << 23),
        name="relay",
    )(inbound[0], jnp.transpose(weights[0], (1, 0, 2)), cotangent[0])
    return out[None]


def solution(mesh):
    sizes = dict(mesh.shape)
    fused = sizes["dp"] == 2 and sizes["tensor"] == 4

    def run(inbound, weights, cotangent):
        if fused and inbound.shape[1] == 2 and weights.shape[3] % 512 == 0 and inbound.shape[2] % 256 == 0:
            return fused_shards(sizes["segment"], inbound, weights, cotangent)
        return shards(inbound, weights, cotangent)

    placed = (
        P("segment", None, "dp", None),
        P("segment", None, None, "tensor"),
        P("segment", None, "dp", "tensor"),
    )
    return jax.shard_map(
        run,
        mesh=mesh,
        in_specs=placed,
        out_specs=P("segment", None, "dp", "tensor"),
        check_vma=False,
    )
```

```python
import jax
import jax.numpy as jnp
from jax import lax
from jax.experimental import pallas as pl
from jax.experimental.pallas import tpu as pltpu
from jax.sharding import PartitionSpec as P

HD = 64


def broadcast(value, axis, root):
    mine = lax.axis_index(axis) == root
    return lax.psum(jnp.where(mine, value, jnp.zeros_like(value)), axis)


def shards(inbound, weights, cotangent):
    states = inbound[0]
    micro_count, row_count, model_width = states.shape
    encoded = broadcast(states, "segment", 0)
    section_layer = weights[0]
    feat_width = section_layer.shape[2]
    head_count = feat_width // HD
    score_scale = HD ** (-0.5)
    query = jnp.dot(
        states.reshape(micro_count * row_count, model_width),
        section_layer[:, 0, :],
        preferred_element_type=jnp.float32,
    ).astype(jnp.bfloat16)
    query = query.reshape(micro_count, row_count, feat_width)
    upstream = cotangent[0]
    pair_weights = section_layer[:, 1:, :].reshape(model_width, 2 * feat_width)
    keyval = jnp.dot(
        encoded.reshape(micro_count * row_count, model_width),
        pair_weights,
        preferred_element_type=jnp.float32,
    ).astype(jnp.bfloat16)
    keyval = keyval.reshape(micro_count, row_count, 2, feat_width)
    all_keyval = lax.all_gather(keyval, "dp", axis=1, tiled=True)
    key_count = all_keyval.shape[1]
    all_query, all_upstream = (query, upstream)
    query_count = all_query.shape[1]

    def attend(items):
        query_one, upstream_one, keyval_one = items
        query_heads = query_one.reshape(query_count, head_count, HD)
        grad_heads = upstream_one.reshape(query_count, head_count, HD)
        key_heads = keyval_one[:, 0].reshape(key_count, head_count, HD)
        value_heads = keyval_one[:, 1].reshape(key_count, head_count, HD)
        scores = (
            jnp.einsum("qhe,khe->hqk", query_heads, key_heads, preferred_element_type=jnp.float32)
            * score_scale
        )
        score_peak = jnp.max(scores, axis=-1, keepdims=True)
        exp_scores = jnp.exp(scores - score_peak)
        attend_prob = exp_scores / jnp.sum(exp_scores, axis=-1, keepdims=True)
        prob_rounded = attend_prob.astype(jnp.bfloat16)
        prob_grad = jnp.einsum(
            "qhe,khe->hqk", grad_heads, value_heads, preferred_element_type=jnp.float32
        )
        row_delta = jnp.sum(attend_prob * prob_grad, axis=-1, keepdims=True)
        score_grad = (attend_prob * (prob_grad - row_delta) * score_scale).astype(jnp.bfloat16)
        context = jnp.einsum(
            "hqk,khe->qhe", prob_rounded, value_heads, preferred_element_type=jnp.float32
        )
        key_grad = jnp.einsum(
            "hqk,qhe->khe", score_grad, query_heads, preferred_element_type=jnp.float32
        )
        value_grad = jnp.einsum(
            "hqk,qhe->khe", prob_rounded, grad_heads, preferred_element_type=jnp.float32
        )
        context = context.astype(jnp.bfloat16).reshape(row_count, feat_width)
        joined = jnp.stack(
            [key_grad.reshape(-1, feat_width), value_grad.reshape(-1, feat_width)], axis=1
        )
        return (context, joined)

    context, joined_grads = lax.map(attend, (all_query, all_upstream, all_keyval))
    owned_grads = lax.psum_scatter(joined_grads, "dp", scatter_dimension=1, tiled=True).astype(
        jnp.bfloat16
    )
    head_terms = jnp.einsum(
        "rc,dc->rd",
        owned_grads.reshape(micro_count * row_count, 2 * feat_width),
        pair_weights,
        preferred_element_type=jnp.float32,
    )
    head_terms = head_terms.reshape(micro_count, row_count, model_width)
    heads_total = lax.psum_scatter(
        head_terms.astype(jnp.bfloat16), "tensor", scatter_dimension=2, tiled=True
    ).astype(jnp.float32)
    segment_index = lax.axis_index("segment")
    live_mask = (segment_index > 0).astype(jnp.float32)
    sections = lax.psum(heads_total * live_mask, "segment")
    encoder_grad = (sections + cotangent[0].astype(jnp.float32)).astype(jnp.bfloat16)
    result = jnp.where(segment_index == 0, encoder_grad, context)
    return result[None]


CHUNKS = 4


def relay_kernel(n_segment, x_ref, w_ref, g_ref, out_ref,
                 enc, own_x, wq, wkv, cot0, parts, ctx, rctx, dkv, rdkv,
                 core_out, core_in, y_out, y_in, total, z_out, z_in,
                 load_x, load_w, load_q, load_g,
                 zs, zr, cs, cr, ys, yr, fs, fr, xs, xr, ds_, dr, ts, tr,
                 ks, kr, vs, vr, us, ur):
    micro, rows, width = x_ref.shape
    feat = w_ref.shape[2]
    half = feat // 2
    quarter = half // 2
    piece = rows // 4
    crow = piece // CHUNKS
    steps = micro * CHUNKS
    zrow = feat // CHUNKS
    pairs = half // 128

    seg = lax.axis_index("segment")
    d = lax.axis_index("dp")
    t = lax.axis_index("tensor")
    y, c = t // 2, t % 2
    peer_x = {"dp": 1 - d}
    peer_c = {"tensor": y * 2 + (1 - c)}
    peer_y = {"tensor": (1 - y) * 2 + c}
    up = {"segment": lax.min(seg + 1, n_segment - 1)}
    down = {"segment": lax.max(seg - 1, 0)}
    first, last = seg == 0, seg == n_segment - 1
    MESH = pl.DeviceIdType.MESH

    def remote(src, dst, s, r, dev):
        return pltpu.make_async_remote_copy(
            src_ref=src, dst_ref=dst, send_sem=s, recv_sem=r,
            device_id=dev, device_id_type=MESH)

    def slot(ref, who, j):
        row = pl.multiple_of(who * piece + lax.rem(j, CHUNKS) * crow, crow)
        return ref.at[j // CHUNKS, pl.ds(row, crow), :]

    def z_copy(ref, j):
        return remote(slot(ref, t, j), slot(enc, t, j), zs.at[j], zr.at[j], up)

    def c_copy(j):
        return remote(slot(enc, t, j), slot(enc, t, j), cs.at[j], cr.at[j], peer_c)

    def y_copy(j):
        return remote(slot(enc, t, j), slot(enc, t, j), ys.at[j], yr.at[j], peer_y)

    ty = (1 - y) * 2 + c

    def f_copy(j):
        return remote(slot(enc, ty, j), slot(enc, ty, j), fs.at[j], fr.at[j], peer_c)

    def lanes(which, size):
        return pl.ds(pl.multiple_of(which * size, size), size)

    def x_copy(kind, m):
        i = kind * micro + m
        return remote(parts.at[kind, m, 2], parts.at[kind, m, d], xs.at[i], xr.at[i], peer_x)

    def g_copy(m):
        i = 3 * micro + m
        return remote(g_ref.at[m, :, lanes(1 - d, half)], parts.at[3, m, d],
                      xs.at[i], xr.at[i], peer_x)

    def g_load(m):
        return pltpu.make_async_copy(g_ref.at[m, :, lanes(d, half)], parts.at[3, m, d], load_g.at[m])

    def q_load(n):
        h = jnp.where(n < 2, 1 - d, d)
        col = pl.multiple_of(h * half + lax.rem(n, 2) * quarter, quarter)
        b = lax.rem(n, 2)
        return pltpu.make_async_copy(w_ref.at[0, :, pl.ds(col, quarter)], wq.at[b], load_q.at[b])

    def w_load(k):
        return pltpu.make_async_copy(w_ref.at[k + 1], wkv.at[k], load_w.at[k])

    def d_copy(m, p):
        i = m * pairs + p
        lane = lanes(p, 128)
        return remote(dkv.at[m, 1 - d, :, :, lane], rdkv.at[m, :, :, lane], ds_.at[i], dr.at[i], peer_x)

    def t_copy(m, p):
        i = m * pairs + p
        lane = lanes(p, 128)
        return remote(ctx.at[m, 1 - d, :, lane], rctx.at[m, :, lane], ts.at[i], tr.at[i], peer_x)

    def k_copy(m, yy):
        i = m * 2 + yy
        return remote(core_out.at[m, yy], core_in.at[m, yy], ks.at[i], kr.at[i], peer_c)

    def v_copy(i):
        m, row = i // CHUNKS, pl.multiple_of(lax.rem(i, CHUNKS) * zrow, zrow)
        return remote(y_out.at[m, pl.ds(row, zrow), :], y_in.at[m, pl.ds(row, zrow), :],
                      vs.at[i], vr.at[i], peer_y)

    def u_copy(i):
        m, row = i // CHUNKS, pl.multiple_of(lax.rem(i, CHUNKS) * zrow, zrow)
        return remote(z_out.at[m, pl.ds(row, zrow), :], z_in.at[m, pl.ds(row, zrow), :],
                      us.at[i], ur.at[i], down)

    x_load = pltpu.make_async_copy(x_ref, own_x, load_x)
    c_load = pltpu.make_async_copy(g_ref, cot0, load_x)

    barrier = pltpu.get_barrier_semaphore()
    for dev in (peer_x, peer_c, peer_y):
        pl.semaphore_signal(barrier, inc=1, device_id=dev, device_id_type=MESH)

    @pl.when(jnp.logical_not(last))
    def _():
        pl.semaphore_signal(barrier, inc=1, device_id=up, device_id_type=MESH)

    @pl.when(jnp.logical_not(first))
    def _():
        pl.semaphore_signal(barrier, inc=1, device_id=down, device_id_type=MESH)

    ends = first.astype(jnp.int32) + last.astype(jnp.int32)
    pl.semaphore_wait(barrier, 5 - ends)

    @pl.when(first)
    def _():
        def send(j, carry):
            z_copy(x_ref, j).start()
            return carry
        lax.fori_loop(0, steps, send, 0)
        c_load.start()
        c_load.wait()

        def finish(i, carry):
            u_copy(i).wait_recv()
            m, row = i // CHUNKS, pl.multiple_of(lax.rem(i, CHUNKS) * zrow, zrow)
            rr = pl.ds(row, zrow)
            out_ref[m, :, rr] = (z_in[m, rr, :].astype(jnp.float32).T
                                 + cot0[m, :, rr].astype(jnp.float32)).astype(out_ref.dtype)
            return carry
        lax.fori_loop(0, steps, finish, 0)

        def drain(j, carry):
            z_copy(x_ref, j).wait_send()
            return carry
        lax.fori_loop(0, steps, drain, 0)

    @pl.when(jnp.logical_not(first))
    def _():
        x_load.start()
        q_load(0).start()
        q_load(1).start()
        for k in range(2):
            w_load(k).start()
        for m in range(micro):
            g_load(m).start()
            g_copy(m).start()

        def forward(j):
            z_copy(enc, j).wait_recv()

            @pl.when(jnp.logical_not(last))
            def _():
                z_copy(enc, j).start()
            y_copy(j).start()
            c_copy(j).start()

        def relay(j):
            y_copy(j).wait_recv()
            f_copy(j).start()

        def q_step(j, carry):
            forward(j)

            @pl.when(j > 0)
            def _():
                relay(j - 1)

            @pl.when(j == 0)
            def _():
                x_load.wait()
            q_load(j).wait()
            value = jnp.dot(own_x[...].reshape(micro * rows, width), wq[lax.rem(j, 2)],
                            preferred_element_type=jnp.float32)
            value = (value * HD ** -0.5).astype(jnp.bfloat16).reshape(micro, rows, quarter)
            where = jnp.where(j < 2, 2, d)
            for m in range(micro):
                parts[0, m, where, :, lanes(lax.rem(j, 2), quarter)] = value[m]

            @pl.when(j < 2)
            def _():
                q_load(j + 2).start()

            @pl.when(j == 1)
            def _():
                for m in range(micro):
                    x_copy(0, m).start()
            return carry
        lax.fori_loop(0, CHUNKS, q_step, 0)
        for k in range(2):
            w_load(k).wait()

        def gathered(m):
            def one(j, carry):
                c_copy(j).wait_recv()
                f_copy(j).wait_recv()
                return carry
            lax.fori_loop(m * CHUNKS, (m + 1) * CHUNKS, one, 0)

        def kv_step(i, carry):
            m, o = i // 4, lax.rem(i, 4)

            @pl.when(m == 0)
            def _():
                forward(CHUNKS + i)
                relay(CHUNKS + i - 1)

            @pl.when(i == 0)
            def _():
                gathered(0)

            @pl.when(i == 4)
            def _():
                relay(steps - 1)
                gathered(1)
            k = lax.rem(o, 2)
            h = jnp.where(o < 2, 1 - d, d)
            value = jnp.dot(enc[m], wkv[k, :, lanes(h, half)], preferred_element_type=jnp.float32)
            parts[1 + k, m, jnp.where(o < 2, 2, d)] = value.astype(jnp.bfloat16)

            @pl.when(o < 2)
            def _():
                x_copy(1 + k, m).start()
            return carry
        lax.fori_loop(0, 4 * micro, kv_step, 0)

        lane_id = lax.broadcasted_iota(jnp.int32, (1, 128), 1)
        f32 = jnp.float32

        def attend(m, lo, hi):
            def pair(p, carry):
                lane = lanes(p, 128)
                key = parts[1, m, 0:2, :, lane].reshape(2 * rows, 128)
                val = parts[2, m, 0:2, :, lane].reshape(2 * rows, 128)
                dk = jnp.zeros((2 * rows, 128), f32)
                dv = jnp.zeros((2 * rows, 128), f32)
                masks = [(lane_id < HD), (lane_id >= HD)]
                zero = jnp.zeros((), jnp.bfloat16)
                for b in range(2):
                    qry = parts[0, m, b, :, lane]
                    ups = parts[3, m, b, :, lane]
                    acc = jnp.zeros((128, rows), f32)
                    for mask in masks:
                        km = jnp.where(mask, key, zero)
                        vm = jnp.where(mask, val, zero)
                        nt = (((1,), (1,)), ((), ()))
                        sc = lax.dot_general(km, qry, nt, preferred_element_type=f32)
                        dp = lax.dot_general(vm, ups, nt, preferred_element_type=f32)
                        ex = jnp.exp(sc - jnp.max(sc, axis=0, keepdims=True))
                        pr = ex * (1.0 / jnp.sum(ex, axis=0, keepdims=True))
                        pb = pr.astype(jnp.bfloat16)
                        delta = jnp.sum(pr * dp, axis=0, keepdims=True)
                        sg = (pr * (dp - delta)).astype(jnp.bfloat16)
                        acc = acc + lax.dot_general(vm, pb, (((0,), (0,)), ((), ())),
                                                    preferred_element_type=f32)
                        dv = dv + jnp.dot(pb, jnp.where(mask, ups, zero), preferred_element_type=f32)
                        dk = dk + jnp.dot(sg, jnp.where(mask, qry, zero), preferred_element_type=f32)
                    ctx[m, b, :, lane] = acc.T.astype(jnp.bfloat16)
                dkb = dk.astype(jnp.bfloat16).reshape(2, rows, 128)
                dvb = dv.astype(jnp.bfloat16).reshape(2, rows, 128)
                for b in range(2):
                    dkv[m, b, 0, :, lane] = dkb[b]
                    dkv[m, b, 1, :, lane] = dvb[b]
                d_copy(m, p).start()
                t_copy(m, p).start()
                return carry
            lax.fori_loop(lo, hi, pair, 0)

        def term(m, col):
            value = None
            for h, ref in ((d, dkv.at[m, d]), (1 - d, rdkv.at[m])):
                for k in range(2):
                    part = lax.dot_general(
                        wkv[k, pl.ds(pl.multiple_of(col, half), half), lanes(h, half)], ref[k],
                        (((1,), (1,)), ((), ())), preferred_element_type=f32)
                    value = part if value is None else value + part
            return value

        def grads_out(m):
            def got(p, carry):
                d_copy(m, p).wait_recv()
                return carry
            lax.fori_loop(0, pairs, got, 0)

            def tile(k, carry):
                yy, o = k // 2, lax.rem(k, 2)
                col = (yy * 2 + 1 - c) * feat + o * half
                core_out[m, yy, lanes(o, half), :] = term(m, col).astype(jnp.bfloat16)

                @pl.when(o == 1)
                def _():
                    k_copy(m, yy).start()
                return carry
            lax.fori_loop(0, 4, tile, 0)

        def grads_in(m):
            def tile(k, carry):
                o = lax.rem(k, 2)
                yy = jnp.where(k < 2, 1 - y, y)

                @pl.when(o == 0)
                def _():
                    k_copy(m, yy).wait_recv()
                col = (yy * 2 + c) * feat + o * half
                value = term(m, col) + core_in[m, yy, lanes(o, half), :].astype(f32)

                @pl.when(k < 2)
                def _():
                    y_out[m, lanes(o, half), :] = value.astype(jnp.bfloat16)
                    for q in range(CHUNKS // 2):
                        v_copy(m * CHUNKS + o * (CHUNKS // 2) + q).start()

                @pl.when(k >= 2)
                def _():
                    total[m, lanes(o, half), :] = value
                return carry
            lax.fori_loop(0, 4, tile, 0)

        def got_parts(m):
            for kind in range(3):
                x_copy(kind, m).wait_recv()
            g_copy(m).wait_recv()
            g_load(m).wait()

        got_parts(0)
        attend(0, 0, pairs)
        got_parts(1)
        attend(1, 0, pairs // 2)
        grads_out(0)
        attend(1, pairs // 2, pairs)
        grads_in(0)
        grads_out(1)
        grads_in(1)

        def chain(i, carry):
            m, row = i // CHUNKS, pl.multiple_of(lax.rem(i, CHUNKS) * zrow, zrow)
            rr = pl.ds(row, zrow)
            v_copy(i).wait_recv()
            total[m, rr, :] = total[m, rr, :] + y_in[m, rr, :].astype(f32)

            @pl.when(jnp.logical_not(last))
            def _():
                u_copy(i).wait_recv()
                total[m, rr, :] = total[m, rr, :] + z_in[m, rr, :].astype(f32)
            z_out[m, rr, :] = total[m, rr, :].astype(jnp.bfloat16)
            u_copy(i).start()
            return carry
        lax.fori_loop(0, steps, chain, 0)

        def context(i, carry):
            t_copy(i // pairs, lax.rem(i, pairs)).wait_recv()
            return carry
        lax.fori_loop(0, micro * pairs, context, 0)
        for m in range(micro):
            out_ref[m, :, lanes(d, half)] = ctx[m, d]
            out_ref[m, :, lanes(1 - d, half)] = rctx[m]

        def drain(i, carry):
            @pl.when(jnp.logical_not(last))
            def _():
                z_copy(enc, i).wait_send()
            c_copy(i).wait_send()
            y_copy(i).wait_send()
            f_copy(i).wait_send()
            v_copy(i).wait_send()
            u_copy(i).wait_send()
            return carry
        lax.fori_loop(0, steps, drain, 0)

        def drain_pairs(i, carry):
            d_copy(i // pairs, lax.rem(i, pairs)).wait_send()
            t_copy(i // pairs, lax.rem(i, pairs)).wait_send()
            return carry
        lax.fori_loop(0, micro * pairs, drain_pairs, 0)
        for m in range(micro):
            for kind in range(3):
                x_copy(kind, m).wait_send()
            g_copy(m).wait_send()
            for yy in range(2):
                k_copy(m, yy).wait_send()


def fused_shards(n_segment, inbound, weights, cotangent):
    micro, rows, width = inbound.shape[1:]
    feat = weights.shape[3]
    half = feat // 2
    steps, pairs = micro * CHUNKS, half // 128
    bf, f32 = jnp.bfloat16, jnp.float32
    vm, dma = pltpu.VMEM, pltpu.SemaphoreType.DMA
    scratch = [
        vm((micro, rows, width), bf),
        vm((micro, rows, width), bf),
        vm((2, width, half // 2), bf),
        vm((2, width, feat), bf),
        vm((micro, rows, feat), bf),
        vm((4, micro, 3, rows, half), bf),
        vm((micro, 2, rows, half), bf),
        vm((micro, rows, half), bf),
        vm((micro, 2, 2, rows, half), bf),
        vm((micro, 2, rows, half), bf),
        vm((micro, 2, feat, rows), bf),
        vm((micro, 2, feat, rows), bf),
        vm((micro, feat, rows), bf),
        vm((micro, feat, rows), bf),
        vm((micro, feat, rows), f32),
        vm((micro, feat, rows), bf),
        vm((micro, feat, rows), bf),
        dma, dma((2,)), dma((2,)), dma((micro,)),
    ]
    scratch += [dma((steps,))] * 8
    scratch += [dma((4 * micro,))] * 2
    scratch += [dma((micro * pairs,))] * 4
    scratch += [dma((2 * micro,))] * 2
    scratch += [dma((steps,))] * 4
    work = 2 * micro * rows * width * feat * 5
    out = pl.pallas_call(
        lambda *refs: relay_kernel(n_segment, *refs),
        out_shape=jax.ShapeDtypeStruct((micro, rows, feat), bf),
        in_specs=[pl.BlockSpec(memory_space=pl.ANY)] * 3,
        out_specs=pl.BlockSpec(memory_space=pltpu.VMEM),
        scratch_shapes=scratch,
        compiler_params=pltpu.CompilerParams(
            collective_id=0, has_side_effects=True, vmem_limit_bytes=62 * 1024 * 1024),
        cost_estimate=pl.CostEstimate(flops=work, bytes_accessed=32 << 20, transcendentals=1 << 23),
        name="relay",
    )(inbound[0], jnp.transpose(weights[0], (1, 0, 2)), cotangent[0])
    return out[None]


def solution(mesh):
    sizes = dict(mesh.shape)
    fused = sizes["dp"] == 2 and sizes["tensor"] == 4

    def run(inbound, weights, cotangent):
        if fused and inbound.shape[1] == 2 and weights.shape[3] % 512 == 0 and inbound.shape[2] % 256 == 0:
            return fused_shards(sizes["segment"], inbound, weights, cotangent)
        return shards(inbound, weights, cotangent)

    placed = (
        P("segment", None, "dp", None),
        P("segment", None, None, "tensor"),
        P("segment", None, "dp", "tensor"),
    )
    return jax.shard_map(
        run,
        mesh=mesh,
        in_specs=placed,
        out_specs=P("segment", None, "dp", "tensor"),
        check_vma=False,
    )
```

```python
import jax
import jax.numpy as jnp
from jax import lax
from jax.experimental import pallas as pl
from jax.experimental.pallas import tpu as pltpu
from jax.sharding import PartitionSpec as P

HD = 64


def broadcast(value, axis, root):
    mine = lax.axis_index(axis) == root
    return lax.psum(jnp.where(mine, value, jnp.zeros_like(value)), axis)


def shards(inbound, weights, cotangent):
    states = inbound[0]
    micro_count, row_count, model_width = states.shape
    encoded = broadcast(states, "segment", 0)
    section_layer = weights[0]
    feat_width = section_layer.shape[2]
    head_count = feat_width // HD
    score_scale = HD ** (-0.5)
    query = jnp.dot(
        states.reshape(micro_count * row_count, model_width),
        section_layer[:, 0, :],
        preferred_element_type=jnp.float32,
    ).astype(jnp.bfloat16)
    query = query.reshape(micro_count, row_count, feat_width)
    upstream = cotangent[0]
    pair_weights = section_layer[:, 1:, :].reshape(model_width, 2 * feat_width)
    keyval = jnp.dot(
        encoded.reshape(micro_count * row_count, model_width),
        pair_weights,
        preferred_element_type=jnp.float32,
    ).astype(jnp.bfloat16)
    keyval = keyval.reshape(micro_count, row_count, 2, feat_width)
    all_keyval = lax.all_gather(keyval, "dp", axis=1, tiled=True)
    key_count = all_keyval.shape[1]
    all_query, all_upstream = (query, upstream)
    query_count = all_query.shape[1]

    def attend(items):
        query_one, upstream_one, keyval_one = items
        query_heads = query_one.reshape(query_count, head_count, HD)
        grad_heads = upstream_one.reshape(query_count, head_count, HD)
        key_heads = keyval_one[:, 0].reshape(key_count, head_count, HD)
        value_heads = keyval_one[:, 1].reshape(key_count, head_count, HD)
        scores = (
            jnp.einsum("qhe,khe->hqk", query_heads, key_heads, preferred_element_type=jnp.float32)
            * score_scale
        )
        score_peak = jnp.max(scores, axis=-1, keepdims=True)
        exp_scores = jnp.exp(scores - score_peak)
        attend_prob = exp_scores / jnp.sum(exp_scores, axis=-1, keepdims=True)
        prob_rounded = attend_prob.astype(jnp.bfloat16)
        prob_grad = jnp.einsum(
            "qhe,khe->hqk", grad_heads, value_heads, preferred_element_type=jnp.float32
        )
        row_delta = jnp.sum(attend_prob * prob_grad, axis=-1, keepdims=True)
        score_grad = (attend_prob * (prob_grad - row_delta) * score_scale).astype(jnp.bfloat16)
        context = jnp.einsum(
            "hqk,khe->qhe", prob_rounded, value_heads, preferred_element_type=jnp.float32
        )
        key_grad = jnp.einsum(
            "hqk,qhe->khe", score_grad, query_heads, preferred_element_type=jnp.float32
        )
        value_grad = jnp.einsum(
            "hqk,qhe->khe", prob_rounded, grad_heads, preferred_element_type=jnp.float32
        )
        context = context.astype(jnp.bfloat16).reshape(row_count, feat_width)
        joined = jnp.stack(
            [key_grad.reshape(-1, feat_width), value_grad.reshape(-1, feat_width)], axis=1
        )
        return (context, joined)

    context, joined_grads = lax.map(attend, (all_query, all_upstream, all_keyval))
    owned_grads = lax.psum_scatter(joined_grads, "dp", scatter_dimension=1, tiled=True).astype(
        jnp.bfloat16
    )
    head_terms = jnp.einsum(
        "rc,dc->rd",
        owned_grads.reshape(micro_count * row_count, 2 * feat_width),
        pair_weights,
        preferred_element_type=jnp.float32,
    )
    head_terms = head_terms.reshape(micro_count, row_count, model_width)
    heads_total = lax.psum_scatter(
        head_terms.astype(jnp.bfloat16), "tensor", scatter_dimension=2, tiled=True
    ).astype(jnp.float32)
    segment_index = lax.axis_index("segment")
    live_mask = (segment_index > 0).astype(jnp.float32)
    sections = lax.psum(heads_total * live_mask, "segment")
    encoder_grad = (sections + cotangent[0].astype(jnp.float32)).astype(jnp.bfloat16)
    result = jnp.where(segment_index == 0, encoder_grad, context)
    return result[None]


CHUNKS = 4


def relay_kernel(n_segment, x_ref, w_ref, g_ref, out_ref,
                 enc, own_x, wq, wkv, cot0, parts, ctx, rctx, dkv, rdkv,
                 core_out, core_in, y_out, y_in, total, z_out, z_in,
                 load_x, load_w, load_q, load_g,
                 zs, zr, cs, cr, ys, yr, fs, fr, xs, xr, ds_, dr, ts, tr,
                 ks, kr, vs, vr, us, ur):
    micro, rows, width = x_ref.shape
    feat = w_ref.shape[2]
    half = feat // 2
    quarter = half // 2
    piece = rows // 4
    crow = piece // CHUNKS
    steps = micro * CHUNKS
    zrow = feat // CHUNKS
    pairs = half // 128

    seg = lax.axis_index("segment")
    d = lax.axis_index("dp")
    t = lax.axis_index("tensor")
    y, c = t // 2, t % 2
    peer_x = {"dp": 1 - d}
    peer_c = {"tensor": y * 2 + (1 - c)}
    peer_y = {"tensor": (1 - y) * 2 + c}
    up = {"segment": lax.min(seg + 1, n_segment - 1)}
    down = {"segment": lax.max(seg - 1, 0)}
    first, last = seg == 0, seg == n_segment - 1
    MESH = pl.DeviceIdType.MESH

    def remote(src, dst, s, r, dev):
        return pltpu.make_async_remote_copy(
            src_ref=src, dst_ref=dst, send_sem=s, recv_sem=r,
            device_id=dev, device_id_type=MESH)

    def slot(ref, who, j):
        row = pl.multiple_of(who * piece + lax.rem(j, CHUNKS) * crow, crow)
        return ref.at[j // CHUNKS, pl.ds(row, crow), :]

    def z_copy(ref, j):
        return remote(slot(ref, t, j), slot(enc, t, j), zs.at[j], zr.at[j], up)

    def c_copy(j):
        return remote(slot(enc, t, j), slot(enc, t, j), cs.at[j], cr.at[j], peer_c)

    def y_copy(j):
        return remote(slot(enc, t, j), slot(enc, t, j), ys.at[j], yr.at[j], peer_y)

    ty = (1 - y) * 2 + c

    def f_copy(j):
        return remote(slot(enc, ty, j), slot(enc, ty, j), fs.at[j], fr.at[j], peer_c)

    def lanes(which, size):
        return pl.ds(pl.multiple_of(which * size, size), size)

    def x_copy(kind, m):
        i = kind * micro + m
        return remote(parts.at[kind, m, 2], parts.at[kind, m, d], xs.at[i], xr.at[i], peer_x)

    def g_copy(m):
        i = 3 * micro + m
        return remote(g_ref.at[m, :, lanes(1 - d, half)], parts.at[3, m, d],
                      xs.at[i], xr.at[i], peer_x)

    def g_load(m):
        return pltpu.make_async_copy(g_ref.at[m, :, lanes(d, half)], parts.at[3, m, d], load_g.at[m])

    def q_load(n):
        h = jnp.where(n < 2, 1 - d, d)
        col = pl.multiple_of(h * half + lax.rem(n, 2) * quarter, quarter)
        b = lax.rem(n, 2)
        return pltpu.make_async_copy(w_ref.at[0, :, pl.ds(col, quarter)], wq.at[b], load_q.at[b])

    def w_load(k):
        return pltpu.make_async_copy(w_ref.at[k + 1], wkv.at[k], load_w.at[k])

    def d_copy(m, p):
        i = m * pairs + p
        lane = lanes(p, 128)
        return remote(dkv.at[m, 1 - d, :, :, lane], rdkv.at[m, :, :, lane], ds_.at[i], dr.at[i], peer_x)

    def t_copy(m, p):
        i = m * pairs + p
        lane = lanes(p, 128)
        return remote(ctx.at[m, 1 - d, :, lane], rctx.at[m, :, lane], ts.at[i], tr.at[i], peer_x)

    def k_copy(m, yy):
        i = m * 2 + yy
        return remote(core_out.at[m, yy], core_in.at[m, yy], ks.at[i], kr.at[i], peer_c)

    def v_copy(i):
        m, row = i // CHUNKS, pl.multiple_of(lax.rem(i, CHUNKS) * zrow, zrow)
        return remote(y_out.at[m, pl.ds(row, zrow), :], y_in.at[m, pl.ds(row, zrow), :],
                      vs.at[i], vr.at[i], peer_y)

    def u_copy(i):
        m, row = i // CHUNKS, pl.multiple_of(lax.rem(i, CHUNKS) * zrow, zrow)
        return remote(z_out.at[m, pl.ds(row, zrow), :], z_in.at[m, pl.ds(row, zrow), :],
                      us.at[i], ur.at[i], down)

    x_load = pltpu.make_async_copy(x_ref, own_x, load_x)
    c_load = pltpu.make_async_copy(g_ref, cot0, load_x)

    barrier = pltpu.get_barrier_semaphore()
    for dev in (peer_x, peer_c, peer_y):
        pl.semaphore_signal(barrier, inc=1, device_id=dev, device_id_type=MESH)

    @pl.when(jnp.logical_not(last))
    def _():
        pl.semaphore_signal(barrier, inc=1, device_id=up, device_id_type=MESH)

    @pl.when(jnp.logical_not(first))
    def _():
        pl.semaphore_signal(barrier, inc=1, device_id=down, device_id_type=MESH)

    ends = first.astype(jnp.int32) + last.astype(jnp.int32)
    pl.semaphore_wait(barrier, 5 - ends)

    @pl.when(first)
    def _():
        def send(j, carry):
            @pl.when(j >= 2)
            def _():
                z_copy(x_ref, j - 2).wait_send()
            z_copy(x_ref, j).start()
            return carry
        lax.fori_loop(0, steps, send, 0)
        c_load.start()
        c_load.wait()

        def finish(i, carry):
            u_copy(i).wait_recv()
            m, row = i // CHUNKS, pl.multiple_of(lax.rem(i, CHUNKS) * zrow, zrow)
            rr = pl.ds(row, zrow)
            out_ref[m, :, rr] = (z_in[m, rr, :].astype(jnp.float32).T
                                 + cot0[m, :, rr].astype(jnp.float32)).astype(out_ref.dtype)
            return carry
        lax.fori_loop(0, steps, finish, 0)

        def drain(j, carry):
            z_copy(x_ref, j).wait_send()
            return carry
        lax.fori_loop(steps - 2, steps, drain, 0)

    @pl.when(jnp.logical_not(first))
    def _():
        x_load.start()
        q_load(0).start()
        q_load(1).start()
        for k in range(2):
            w_load(k).start()
        for m in range(micro):
            g_load(m).start()
            g_copy(m).start()

        def forward(j):
            z_copy(enc, j).wait_recv()

            @pl.when(jnp.logical_not(last))
            def _():
                z_copy(enc, j).start()
            y_copy(j).start()
            c_copy(j).start()

        def relay(j):
            y_copy(j).wait_recv()
            f_copy(j).start()

        def q_step(j, carry):
            forward(j)

            @pl.when(j > 0)
            def _():
                relay(j - 1)

            @pl.when(j == 0)
            def _():
                x_load.wait()
            q_load(j).wait()
            value = jnp.dot(own_x[...].reshape(micro * rows, width), wq[lax.rem(j, 2)],
                            preferred_element_type=jnp.float32)
            value = (value * HD ** -0.5).astype(jnp.bfloat16).reshape(micro, rows, quarter)
            where = jnp.where(j < 2, 2, d)
            for m in range(micro):
                parts[0, m, where, :, lanes(lax.rem(j, 2), quarter)] = value[m]

            @pl.when(j < 2)
            def _():
                q_load(j + 2).start()

            @pl.when(j == 1)
            def _():
                for m in range(micro):
                    x_copy(0, m).start()
            return carry
        lax.fori_loop(0, CHUNKS, q_step, 0)
        for k in range(2):
            w_load(k).wait()

        def gathered(m):
            def one(j, carry):
                c_copy(j).wait_recv()
                f_copy(j).wait_recv()
                return carry
            lax.fori_loop(m * CHUNKS, (m + 1) * CHUNKS, one, 0)

        def kv_step(i, carry):
            m, o = i // 4, lax.rem(i, 4)

            @pl.when(m == 0)
            def _():
                forward(CHUNKS + i)
                relay(CHUNKS + i - 1)

            @pl.when(i == 0)
            def _():
                gathered(0)

            @pl.when(i == 4)
            def _():
                relay(steps - 1)
                gathered(1)
            k = lax.rem(o, 2)
            h = jnp.where(o < 2, 1 - d, d)
            value = jnp.dot(enc[m], wkv[k, :, lanes(h, half)], preferred_element_type=jnp.float32)
            parts[1 + k, m, jnp.where(o < 2, 2, d)] = value.astype(jnp.bfloat16)

            @pl.when(o < 2)
            def _():
                x_copy(1 + k, m).start()
            return carry
        lax.fori_loop(0, 4 * micro, kv_step, 0)

        lane_id = lax.broadcasted_iota(jnp.int32, (1, 128), 1)
        f32 = jnp.float32

        def attend(m, lo, hi):
            def pair(p, carry):
                lane = lanes(p, 128)
                key = parts[1, m, 0:2, :, lane].reshape(2 * rows, 128)
                val = parts[2, m, 0:2, :, lane].reshape(2 * rows, 128)
                dk = jnp.zeros((2 * rows, 128), f32)
                dv = jnp.zeros((2 * rows, 128), f32)
                masks = [(lane_id < HD), (lane_id >= HD)]
                zero = jnp.zeros((), jnp.bfloat16)
                for b in range(2):
                    qry = parts[0, m, b, :, lane]
                    ups = parts[3, m, b, :, lane]
                    acc = jnp.zeros((128, rows), f32)
                    for mask in masks:
                        km = jnp.where(mask, key, zero)
                        vm = jnp.where(mask, val, zero)
                        nt = (((1,), (1,)), ((), ()))
                        sc = lax.dot_general(km, qry, nt, preferred_element_type=f32)
                        dp = lax.dot_general(vm, ups, nt, preferred_element_type=f32)
                        ex = jnp.exp(sc - jnp.max(sc, axis=0, keepdims=True))
                        pr = ex * (1.0 / jnp.sum(ex, axis=0, keepdims=True))
                        pb = pr.astype(jnp.bfloat16)
                        delta = jnp.sum(pr * dp, axis=0, keepdims=True)
                        sg = (pr * (dp - delta)).astype(jnp.bfloat16)
                        acc = acc + lax.dot_general(vm, pb, (((0,), (0,)), ((), ())),
                                                    preferred_element_type=f32)
                        dv = dv + jnp.dot(pb, jnp.where(mask, ups, zero), preferred_element_type=f32)
                        dk = dk + jnp.dot(sg, jnp.where(mask, qry, zero), preferred_element_type=f32)
                    ctx[m, b, :, lane] = acc.T.astype(jnp.bfloat16)
                dkb = dk.astype(jnp.bfloat16).reshape(2, rows, 128)
                dvb = dv.astype(jnp.bfloat16).reshape(2, rows, 128)
                for b in range(2):
                    dkv[m, b, 0, :, lane] = dkb[b]
                    dkv[m, b, 1, :, lane] = dvb[b]
                d_copy(m, p).start()
                return carry
            lax.fori_loop(lo, hi, pair, 0)

        def term(m, col):
            value = None
            for h, ref in ((d, dkv.at[m, d]), (1 - d, rdkv.at[m])):
                for k in range(2):
                    part = lax.dot_general(
                        wkv[k, pl.ds(pl.multiple_of(col, half), half), lanes(h, half)], ref[k],
                        (((1,), (1,)), ((), ())), preferred_element_type=f32)
                    value = part if value is None else value + part
            return value

        def got_grads(m):
            def got(p, carry):
                d_copy(m, p).wait_recv()
                return carry
            lax.fori_loop(0, pairs, got, 0)

        def grads_out(m, yy):
            def tile(o, carry):
                col = (yy * 2 + 1 - c) * feat + o * half
                core_out[m, yy, lanes(o, half), :] = term(m, col).astype(jnp.bfloat16)
                return carry
            lax.fori_loop(0, 2, tile, 0)
            k_copy(m, yy).start()

        def grads_far(m):
            k_copy(m, 1 - y).wait_recv()

            def tile(o, carry):
                col = ((1 - y) * 2 + c) * feat + o * half
                value = term(m, col) + core_in[m, 1 - y, lanes(o, half), :].astype(f32)
                y_out[m, lanes(o, half), :] = value.astype(jnp.bfloat16)

                @pl.when(o == 0)
                def _():
                    for q in range(CHUNKS // 2):
                        v_copy(m * CHUNKS + q).start()
                return carry
            lax.fori_loop(0, 2, tile, 0)

        def grads_near(m):
            k_copy(m, y).wait_recv()

            def tile(o, carry):
                col = (y * 2 + c) * feat + o * half
                value = term(m, col) + core_in[m, y, lanes(o, half), :].astype(f32)
                total[m, lanes(o, half), :] = value
                return carry
            lax.fori_loop(0, 2, tile, 0)

        def far_rest(m):
            for q in range(CHUNKS // 2):
                v_copy(m * CHUNKS + q).wait_send()
                v_copy(m * CHUNKS + CHUNKS // 2 + q).start()

        def got_parts(m):
            for kind in range(3):
                x_copy(kind, m).wait_recv()
            g_copy(m).wait_recv()
            g_load(m).wait()

        got_parts(0)
        attend(0, 0, pairs)
        got_parts(1)
        attend(1, 0, pairs // 2)
        got_grads(0)
        grads_out(0, 1 - y)
        grads_out(0, y)
        grads_far(0)
        grads_near(0)
        attend(1, pairs // 2, pairs - 1)
        far_rest(0)
        attend(1, pairs - 1, pairs)

        def chain(i, carry):
            m, row = i // CHUNKS, pl.multiple_of(lax.rem(i, CHUNKS) * zrow, zrow)
            rr = pl.ds(row, zrow)
            v_copy(i).wait_recv()
            value = total[m, rr, :] + y_in[m, rr, :].astype(f32)
            total[m, rr, :] = value

            @pl.when(jnp.logical_not(last))
            def _():
                u_copy(i).wait_recv()
                total[m, rr, :] = total[m, rr, :] + z_in[m, rr, :].astype(f32)
            z_out[m, rr, :] = total[m, rr, :].astype(jnp.bfloat16)

            @pl.when(i >= 2)
            def _():
                u_copy(i - 2).wait_send()
            u_copy(i).start()
            return carry

        got_grads(1)
        grads_out(1, 1 - y)
        grads_far(1)
        lax.fori_loop(0, CHUNKS // 2, chain, 0)
        grads_out(1, y)
        lax.fori_loop(CHUNKS // 2, CHUNKS, chain, 0)
        grads_near(1)
        far_rest(1)

        def context_out(i, carry):
            t_copy(i // pairs, lax.rem(i, pairs)).start()
            return carry
        lax.fori_loop(0, micro * pairs, context_out, 0)
        lax.fori_loop(CHUNKS, steps, chain, 0)

        def context(i, carry):
            t_copy(i // pairs, lax.rem(i, pairs)).wait_recv()
            return carry
        lax.fori_loop(0, micro * pairs, context, 0)
        for m in range(micro):
            out_ref[m, :, lanes(d, half)] = ctx[m, d]
            out_ref[m, :, lanes(1 - d, half)] = rctx[m]

        def drain(i, carry):
            @pl.when(jnp.logical_not(last))
            def _():
                z_copy(enc, i).wait_send()
            c_copy(i).wait_send()
            y_copy(i).wait_send()
            f_copy(i).wait_send()
            return carry
        lax.fori_loop(0, steps, drain, 0)
        for m in range(micro):
            for q in range(CHUNKS // 2):
                v_copy(m * CHUNKS + CHUNKS // 2 + q).wait_send()
        for i in range(steps - 2, steps):
            u_copy(i).wait_send()

        def drain_pairs(i, carry):
            d_copy(i // pairs, lax.rem(i, pairs)).wait_send()
            t_copy(i // pairs, lax.rem(i, pairs)).wait_send()
            return carry
        lax.fori_loop(0, micro * pairs, drain_pairs, 0)
        for m in range(micro):
            for kind in range(3):
                x_copy(kind, m).wait_send()
            g_copy(m).wait_send()
            for yy in range(2):
                k_copy(m, yy).wait_send()


def fused_shards(n_segment, inbound, weights, cotangent):
    micro, rows, width = inbound.shape[1:]
    feat = weights.shape[3]
    half = feat // 2
    steps, pairs = micro * CHUNKS, half // 128
    bf, f32 = jnp.bfloat16, jnp.float32
    vm, dma = pltpu.VMEM, pltpu.SemaphoreType.DMA
    scratch = [
        vm((micro, rows, width), bf),
        vm((micro, rows, width), bf),
        vm((2, width, half // 2), bf),
        vm((2, width, feat), bf),
        vm((micro, rows, feat), bf),
        vm((4, micro, 3, rows, half), bf),
        vm((micro, 2, rows, half), bf),
        vm((micro, rows, half), bf),
        vm((micro, 2, 2, rows, half), bf),
        vm((micro, 2, rows, half), bf),
        vm((micro, 2, feat, rows), bf),
        vm((micro, 2, feat, rows), bf),
        vm((micro, feat, rows), bf),
        vm((micro, feat, rows), bf),
        vm((micro, feat, rows), f32),
        vm((micro, feat, rows), bf),
        vm((micro, feat, rows), bf),
        dma, dma((2,)), dma((2,)), dma((micro,)),
    ]
    scratch += [dma((steps,))] * 8
    scratch += [dma((4 * micro,))] * 2
    scratch += [dma((micro * pairs,))] * 4
    scratch += [dma((2 * micro,))] * 2
    scratch += [dma((steps,))] * 4
    work = 2 * micro * rows * width * feat * 5
    out = pl.pallas_call(
        lambda *refs: relay_kernel(n_segment, *refs),
        out_shape=jax.ShapeDtypeStruct((micro, rows, feat), bf),
        in_specs=[pl.BlockSpec(memory_space=pl.ANY)] * 3,
        out_specs=pl.BlockSpec(memory_space=pltpu.VMEM),
        scratch_shapes=scratch,
        compiler_params=pltpu.CompilerParams(
            collective_id=0, has_side_effects=True, vmem_limit_bytes=62 * 1024 * 1024),
        cost_estimate=pl.CostEstimate(flops=work, bytes_accessed=32 << 20, transcendentals=1 << 23),
        name="relay",
    )(inbound[0], jnp.transpose(weights[0], (1, 0, 2)), cotangent[0])
    return out[None]


def solution(mesh):
    sizes = dict(mesh.shape)
    fused = sizes["dp"] == 2 and sizes["tensor"] == 4

    def run(inbound, weights, cotangent):
        if fused and inbound.shape[1] == 2 and weights.shape[3] % 512 == 0 and inbound.shape[2] % 256 == 0:
            return fused_shards(sizes["segment"], inbound, weights, cotangent)
        return shards(inbound, weights, cotangent)

    placed = (
        P("segment", None, "dp", None),
        P("segment", None, None, "tensor"),
        P("segment", None, "dp", "tensor"),
    )
    return jax.shard_map(
        run,
        mesh=mesh,
        in_specs=placed,
        out_specs=P("segment", None, "dp", "tensor"),
        check_vma=False,
    )
```

```python
import jax
import jax.numpy as jnp
from jax import lax
from jax.experimental import pallas as pl
from jax.experimental.pallas import tpu as pltpu
from jax.sharding import PartitionSpec as P

HD = 64


def broadcast(value, axis, root):
    mine = lax.axis_index(axis) == root
    return lax.psum(jnp.where(mine, value, jnp.zeros_like(value)), axis)


def shards(inbound, weights, cotangent):
    states = inbound[0]
    micro_count, row_count, model_width = states.shape
    encoded = broadcast(states, "segment", 0)
    section_layer = weights[0]
    feat_width = section_layer.shape[2]
    head_count = feat_width // HD
    score_scale = HD ** (-0.5)
    query = jnp.dot(
        states.reshape(micro_count * row_count, model_width),
        section_layer[:, 0, :],
        preferred_element_type=jnp.float32,
    ).astype(jnp.bfloat16)
    query = query.reshape(micro_count, row_count, feat_width)
    upstream = cotangent[0]
    pair_weights = section_layer[:, 1:, :].reshape(model_width, 2 * feat_width)
    keyval = jnp.dot(
        encoded.reshape(micro_count * row_count, model_width),
        pair_weights,
        preferred_element_type=jnp.float32,
    ).astype(jnp.bfloat16)
    keyval = keyval.reshape(micro_count, row_count, 2, feat_width)
    all_keyval = lax.all_gather(keyval, "dp", axis=1, tiled=True)
    key_count = all_keyval.shape[1]
    all_query, all_upstream = (query, upstream)
    query_count = all_query.shape[1]

    def attend(items):
        query_one, upstream_one, keyval_one = items
        query_heads = query_one.reshape(query_count, head_count, HD)
        grad_heads = upstream_one.reshape(query_count, head_count, HD)
        key_heads = keyval_one[:, 0].reshape(key_count, head_count, HD)
        value_heads = keyval_one[:, 1].reshape(key_count, head_count, HD)
        scores = (
            jnp.einsum("qhe,khe->hqk", query_heads, key_heads, preferred_element_type=jnp.float32)
            * score_scale
        )
        score_peak = jnp.max(scores, axis=-1, keepdims=True)
        exp_scores = jnp.exp(scores - score_peak)
        attend_prob = exp_scores / jnp.sum(exp_scores, axis=-1, keepdims=True)
        prob_rounded = attend_prob.astype(jnp.bfloat16)
        prob_grad = jnp.einsum(
            "qhe,khe->hqk", grad_heads, value_heads, preferred_element_type=jnp.float32
        )
        row_delta = jnp.sum(attend_prob * prob_grad, axis=-1, keepdims=True)
        score_grad = (attend_prob * (prob_grad - row_delta) * score_scale).astype(jnp.bfloat16)
        context = jnp.einsum(
            "hqk,khe->qhe", prob_rounded, value_heads, preferred_element_type=jnp.float32
        )
        key_grad = jnp.einsum(
            "hqk,qhe->khe", score_grad, query_heads, preferred_element_type=jnp.float32
        )
        value_grad = jnp.einsum(
            "hqk,qhe->khe", prob_rounded, grad_heads, preferred_element_type=jnp.float32
        )
        context = context.astype(jnp.bfloat16).reshape(row_count, feat_width)
        joined = jnp.stack(
            [key_grad.reshape(-1, feat_width), value_grad.reshape(-1, feat_width)], axis=1
        )
        return (context, joined)

    context, joined_grads = lax.map(attend, (all_query, all_upstream, all_keyval))
    owned_grads = lax.psum_scatter(joined_grads, "dp", scatter_dimension=1, tiled=True).astype(
        jnp.bfloat16
    )
    head_terms = jnp.einsum(
        "rc,dc->rd",
        owned_grads.reshape(micro_count * row_count, 2 * feat_width),
        pair_weights,
        preferred_element_type=jnp.float32,
    )
    head_terms = head_terms.reshape(micro_count, row_count, model_width)
    heads_total = lax.psum_scatter(
        head_terms.astype(jnp.bfloat16), "tensor", scatter_dimension=2, tiled=True
    ).astype(jnp.float32)
    segment_index = lax.axis_index("segment")
    live_mask = (segment_index > 0).astype(jnp.float32)
    sections = lax.psum(heads_total * live_mask, "segment")
    encoder_grad = (sections + cotangent[0].astype(jnp.float32)).astype(jnp.bfloat16)
    result = jnp.where(segment_index == 0, encoder_grad, context)
    return result[None]


CHUNKS = 4


def relay_kernel(n_segment, x_ref, w_ref, g_ref, out_ref,
                 enc, own_x, wq, wkv, cot0, parts, ctx, rctx, dkv, rdkv,
                 core_out, core_in, y_out, y_in, total, z_out, z_in,
                 load_x, load_w, load_q, load_g,
                 zs, zr, cs, cr, ys, yr, fs, fr, xs, xr, ds_, dr, ts, tr,
                 ks, kr, vs, vr, us, ur):
    micro, rows, width = x_ref.shape
    feat = w_ref.shape[2]
    half = feat // 2
    quarter = half // 2
    piece = rows // 4
    crow = piece // CHUNKS
    steps = micro * CHUNKS
    zrow = feat // CHUNKS
    pairs = half // 128

    seg = lax.axis_index("segment")
    d = lax.axis_index("dp")
    t = lax.axis_index("tensor")
    y, c = t // 2, t % 2
    peer_x = {"dp": 1 - d}
    peer_c = {"tensor": y * 2 + (1 - c)}
    peer_y = {"tensor": (1 - y) * 2 + c}
    up = {"segment": lax.min(seg + 1, n_segment - 1)}
    down = {"segment": lax.max(seg - 1, 0)}
    first, last = seg == 0, seg == n_segment - 1
    MESH = pl.DeviceIdType.MESH

    def remote(src, dst, s, r, dev):
        return pltpu.make_async_remote_copy(
            src_ref=src, dst_ref=dst, send_sem=s, recv_sem=r,
            device_id=dev, device_id_type=MESH)

    def slot(ref, who, j):
        row = pl.multiple_of(who * piece + lax.rem(j, CHUNKS) * crow, crow)
        return ref.at[j // CHUNKS, pl.ds(row, crow), :]

    def z_copy(ref, j):
        return remote(slot(ref, t, j), slot(enc, t, j), zs.at[j], zr.at[j], up)

    def c_copy(j):
        return remote(slot(enc, t, j), slot(enc, t, j), cs.at[j], cr.at[j], peer_c)

    def y_copy(j):
        return remote(slot(enc, t, j), slot(enc, t, j), ys.at[j], yr.at[j], peer_y)

    ty = (1 - y) * 2 + c

    def f_copy(j):
        return remote(slot(enc, ty, j), slot(enc, ty, j), fs.at[j], fr.at[j], peer_c)

    def lanes(which, size):
        return pl.ds(pl.multiple_of(which * size, size), size)

    def x_copy(kind, m):
        i = kind * micro + m
        return remote(parts.at[kind, m, 2], parts.at[kind, m, d], xs.at[i], xr.at[i], peer_x)

    def g_copy(m):
        i = 3 * micro + m
        return remote(g_ref.at[m, :, lanes(1 - d, half)], parts.at[3, m, d],
                      xs.at[i], xr.at[i], peer_x)

    def g_load(m):
        return pltpu.make_async_copy(g_ref.at[m, :, lanes(d, half)], parts.at[3, m, d], load_g.at[m])

    def q_load(n):
        h = jnp.where(n < 2, 1 - d, d)
        col = pl.multiple_of(h * half + lax.rem(n, 2) * quarter, quarter)
        b = lax.rem(n, 2)
        return pltpu.make_async_copy(w_ref.at[0, :, pl.ds(col, quarter)], wq.at[b], load_q.at[b])

    def w_load(k):
        return pltpu.make_async_copy(w_ref.at[k + 1], wkv.at[k], load_w.at[k])

    def d_copy(m, p):
        i = m * pairs + p
        lane = lanes(p, 128)
        return remote(dkv.at[m, 1 - d, :, :, lane], rdkv.at[m, :, :, lane], ds_.at[i], dr.at[i], peer_x)

    def t_copy(m, p):
        i = m * pairs + p
        lane = lanes(p, 128)
        return remote(ctx.at[m, 1 - d, :, lane], rctx.at[m, :, lane], ts.at[i], tr.at[i], peer_x)

    def k_copy(m, yy):
        i = m * 2 + yy
        return remote(core_out.at[m, yy], core_in.at[m, yy], ks.at[i], kr.at[i], peer_c)

    def v_copy(i):
        m, row = i // CHUNKS, pl.multiple_of(lax.rem(i, CHUNKS) * zrow, zrow)
        return remote(y_out.at[m, pl.ds(row, zrow), :], y_in.at[m, pl.ds(row, zrow), :],
                      vs.at[i], vr.at[i], peer_y)

    def u_copy(i):
        m, row = i // CHUNKS, pl.multiple_of(lax.rem(i, CHUNKS) * zrow, zrow)
        return remote(z_out.at[m, pl.ds(row, zrow), :], z_in.at[m, pl.ds(row, zrow), :],
                      us.at[i], ur.at[i], down)

    x_load = pltpu.make_async_copy(x_ref, own_x, load_x)
    c_load = pltpu.make_async_copy(g_ref, cot0, load_x)

    barrier = pltpu.get_barrier_semaphore()
    for dev in (peer_x, peer_c, peer_y):
        pl.semaphore_signal(barrier, inc=1, device_id=dev, device_id_type=MESH)

    @pl.when(jnp.logical_not(last))
    def _():
        pl.semaphore_signal(barrier, inc=1, device_id=up, device_id_type=MESH)

    @pl.when(jnp.logical_not(first))
    def _():
        pl.semaphore_signal(barrier, inc=1, device_id=down, device_id_type=MESH)

    ends = first.astype(jnp.int32) + last.astype(jnp.int32)
    pl.semaphore_wait(barrier, 5 - ends)

    @pl.when(first)
    def _():
        def send(j, carry):
            @pl.when(j >= 2)
            def _():
                z_copy(x_ref, j - 2).wait_send()
            z_copy(x_ref, j).start()
            return carry
        lax.fori_loop(0, steps, send, 0)
        c_load.start()
        c_load.wait()

        def finish(i, carry):
            u_copy(i).wait_recv()
            m, row = i // CHUNKS, pl.multiple_of(lax.rem(i, CHUNKS) * zrow, zrow)
            rr = pl.ds(row, zrow)
            out_ref[m, :, rr] = (z_in[m, rr, :].astype(jnp.float32).T
                                 + cot0[m, :, rr].astype(jnp.float32)).astype(out_ref.dtype)
            return carry
        lax.fori_loop(0, steps, finish, 0)

        def drain(j, carry):
            z_copy(x_ref, j).wait_send()
            return carry
        lax.fori_loop(steps - 2, steps, drain, 0)

    @pl.when(jnp.logical_not(first))
    def _():
        x_load.start()
        q_load(0).start()
        q_load(1).start()
        for k in range(2):
            w_load(k).start()
        for m in range(micro):
            g_load(m).start()
            g_copy(m).start()

        def forward(j):
            z_copy(enc, j).wait_recv()

            @pl.when(jnp.logical_not(last))
            def _():
                z_copy(enc, j).start()
            y_copy(j).start()
            c_copy(j).start()

        def relay(j):
            y_copy(j).wait_recv()
            f_copy(j).start()

        def q_step(j, carry):
            forward(j)

            @pl.when(j > 0)
            def _():
                relay(j - 1)

            @pl.when(j == 0)
            def _():
                x_load.wait()
            q_load(j).wait()
            value = jnp.dot(own_x[...].reshape(micro * rows, width), wq[lax.rem(j, 2)],
                            preferred_element_type=jnp.float32)
            value = (value * HD ** -0.5).astype(jnp.bfloat16).reshape(micro, rows, quarter)
            where = jnp.where(j < 2, 2, d)
            for m in range(micro):
                parts[0, m, where, :, lanes(lax.rem(j, 2), quarter)] = value[m]

            @pl.when(j < 2)
            def _():
                q_load(j + 2).start()

            @pl.when(j == 1)
            def _():
                for m in range(micro):
                    x_copy(0, m).start()
            return carry
        lax.fori_loop(0, CHUNKS, q_step, 0)
        for k in range(2):
            w_load(k).wait()

        def gathered(m):
            def one(j, carry):
                c_copy(j).wait_recv()
                f_copy(j).wait_recv()
                return carry
            lax.fori_loop(m * CHUNKS, (m + 1) * CHUNKS, one, 0)

        def kv_step(i, carry):
            m, o = i // 4, lax.rem(i, 4)

            @pl.when(m == 0)
            def _():
                forward(CHUNKS + i)
                relay(CHUNKS + i - 1)

            @pl.when(i == 0)
            def _():
                gathered(0)

            @pl.when(i == 4)
            def _():
                relay(steps - 1)
                gathered(1)
            k = lax.rem(o, 2)
            h = jnp.where(o < 2, 1 - d, d)
            value = jnp.dot(enc[m], wkv[k, :, lanes(h, half)], preferred_element_type=jnp.float32)
            parts[1 + k, m, jnp.where(o < 2, 2, d)] = value.astype(jnp.bfloat16)

            @pl.when(o < 2)
            def _():
                x_copy(1 + k, m).start()
            return carry
        lax.fori_loop(0, 4 * micro, kv_step, 0)

        lane_id = lax.broadcasted_iota(jnp.int32, (1, 128), 1)
        f32 = jnp.float32

        def attend(m, lo, hi):
            def pair(p, carry):
                lane = lanes(p, 128)
                key = parts[1, m, 0:2, :, lane].reshape(2 * rows, 128)
                val = parts[2, m, 0:2, :, lane].reshape(2 * rows, 128)
                zero = jnp.zeros((), jnp.bfloat16)
                masks = [(lane_id < HD), (lane_id >= HD)]
                keys = [jnp.where(mask, key, zero) for mask in masks]
                vals = [jnp.where(mask, val, zero) for mask in masks]
                both = jnp.concatenate(vals, axis=0)
                probs, grads, qrys, upss = [], [], [], []
                nt = (((1,), (1,)), ((), ()))
                for b in range(2):
                    qry = parts[0, m, b, :, lane]
                    ups = parts[3, m, b, :, lane]
                    for mask, km, vm in zip(masks, keys, vals):
                        sc = lax.dot_general(km, qry, nt, preferred_element_type=f32)
                        dp = lax.dot_general(vm, ups, nt, preferred_element_type=f32)
                        ex = jnp.exp(sc - jnp.max(sc, axis=0, keepdims=True))
                        pr = ex * (1.0 / jnp.sum(ex, axis=0, keepdims=True))
                        delta = jnp.sum(pr * dp, axis=0, keepdims=True)
                        probs.append(pr.astype(jnp.bfloat16))
                        grads.append((pr * (dp - delta)).astype(jnp.bfloat16))
                        qrys.append(jnp.where(mask, qry, zero))
                        upss.append(jnp.where(mask, ups, zero))
                    acc = lax.dot_general(both, jnp.concatenate(probs[-2:], axis=0),
                                          (((0,), (0,)), ((), ())), preferred_element_type=f32)
                    ctx[m, b, :, lane] = acc.T.astype(jnp.bfloat16)
                dv = jnp.dot(jnp.concatenate(probs, axis=1), jnp.concatenate(upss, axis=0),
                             preferred_element_type=f32)
                dk = jnp.dot(jnp.concatenate(grads, axis=1), jnp.concatenate(qrys, axis=0),
                             preferred_element_type=f32)
                dkb = dk.astype(jnp.bfloat16).reshape(2, rows, 128)
                dvb = dv.astype(jnp.bfloat16).reshape(2, rows, 128)
                for b in range(2):
                    dkv[m, b, 0, :, lane] = dkb[b]
                    dkv[m, b, 1, :, lane] = dvb[b]
                d_copy(m, p).start()
                return carry
            lax.fori_loop(lo, hi, pair, 0)

        def term(m, col):
            value = None
            for h, ref in ((d, dkv.at[m, d]), (1 - d, rdkv.at[m])):
                for k in range(2):
                    part = lax.dot_general(
                        wkv[k, pl.ds(pl.multiple_of(col, half), half), lanes(h, half)], ref[k],
                        (((1,), (1,)), ((), ())), preferred_element_type=f32)
                    value = part if value is None else value + part
            return value

        def got_grads(m):
            def got(p, carry):
                d_copy(m, p).wait_recv()
                return carry
            lax.fori_loop(0, pairs, got, 0)

        def grads_out(m, yy):
            def tile(o, carry):
                col = (yy * 2 + 1 - c) * feat + o * half
                core_out[m, yy, lanes(o, half), :] = term(m, col).astype(jnp.bfloat16)
                return carry
            lax.fori_loop(0, 2, tile, 0)
            k_copy(m, yy).start()

        def grads_far(m):
            k_copy(m, 1 - y).wait_recv()

            def tile(o, carry):
                col = ((1 - y) * 2 + c) * feat + o * half
                value = term(m, col) + core_in[m, 1 - y, lanes(o, half), :].astype(f32)
                y_out[m, lanes(o, half), :] = value.astype(jnp.bfloat16)

                @pl.when(o == 0)
                def _():
                    for q in range(CHUNKS // 2):
                        v_copy(m * CHUNKS + q).start()
                return carry
            lax.fori_loop(0, 2, tile, 0)

        def grads_near(m):
            k_copy(m, y).wait_recv()

            def tile(o, carry):
                col = (y * 2 + c) * feat + o * half
                value = term(m, col) + core_in[m, y, lanes(o, half), :].astype(f32)
                total[m, lanes(o, half), :] = value
                return carry
            lax.fori_loop(0, 2, tile, 0)

        def far_rest(m):
            for q in range(CHUNKS // 2):
                v_copy(m * CHUNKS + q).wait_send()
                v_copy(m * CHUNKS + CHUNKS // 2 + q).start()

        def got_parts(m):
            for kind in range(3):
                x_copy(kind, m).wait_recv()
            g_copy(m).wait_recv()
            g_load(m).wait()

        got_parts(0)
        attend(0, 0, pairs)
        got_parts(1)
        attend(1, 0, pairs // 2)
        got_grads(0)
        grads_out(0, 1 - y)
        grads_out(0, y)
        grads_far(0)
        grads_near(0)
        attend(1, pairs // 2, pairs - 1)
        far_rest(0)
        attend(1, pairs - 1, pairs)

        def chain(i, carry):
            m, row = i // CHUNKS, pl.multiple_of(lax.rem(i, CHUNKS) * zrow, zrow)
            rr = pl.ds(row, zrow)
            v_copy(i).wait_recv()
            value = total[m, rr, :] + y_in[m, rr, :].astype(f32)
            total[m, rr, :] = value

            @pl.when(jnp.logical_not(last))
            def _():
                u_copy(i).wait_recv()
                total[m, rr, :] = total[m, rr, :] + z_in[m, rr, :].astype(f32)
            z_out[m, rr, :] = total[m, rr, :].astype(jnp.bfloat16)

            @pl.when(i >= 2)
            def _():
                u_copy(i - 2).wait_send()
            u_copy(i).start()
            return carry

        got_grads(1)
        grads_out(1, 1 - y)
        grads_far(1)
        lax.fori_loop(0, CHUNKS // 2, chain, 0)
        grads_out(1, y)
        lax.fori_loop(CHUNKS // 2, CHUNKS, chain, 0)
        grads_near(1)
        far_rest(1)

        def context_out(i, carry):
            t_copy(i // pairs, lax.rem(i, pairs)).start()
            return carry
        lax.fori_loop(0, micro * pairs, context_out, 0)
        lax.fori_loop(CHUNKS, steps, chain, 0)

        def context(i, carry):
            t_copy(i // pairs, lax.rem(i, pairs)).wait_recv()
            return carry
        lax.fori_loop(0, micro * pairs, context, 0)
        for m in range(micro):
            out_ref[m, :, lanes(d, half)] = ctx[m, d]
            out_ref[m, :, lanes(1 - d, half)] = rctx[m]

        def drain(i, carry):
            @pl.when(jnp.logical_not(last))
            def _():
                z_copy(enc, i).wait_send()
            c_copy(i).wait_send()
            y_copy(i).wait_send()
            f_copy(i).wait_send()
            return carry
        lax.fori_loop(0, steps, drain, 0)
        for m in range(micro):
            for q in range(CHUNKS // 2):
                v_copy(m * CHUNKS + CHUNKS // 2 + q).wait_send()
        for i in range(steps - 2, steps):
            u_copy(i).wait_send()

        def drain_pairs(i, carry):
            d_copy(i // pairs, lax.rem(i, pairs)).wait_send()
            t_copy(i // pairs, lax.rem(i, pairs)).wait_send()
            return carry
        lax.fori_loop(0, micro * pairs, drain_pairs, 0)
        for m in range(micro):
            for kind in range(3):
                x_copy(kind, m).wait_send()
            g_copy(m).wait_send()
            for yy in range(2):
                k_copy(m, yy).wait_send()


def fused_shards(n_segment, inbound, weights, cotangent):
    micro, rows, width = inbound.shape[1:]
    feat = weights.shape[3]
    half = feat // 2
    steps, pairs = micro * CHUNKS, half // 128
    bf, f32 = jnp.bfloat16, jnp.float32
    vm, dma = pltpu.VMEM, pltpu.SemaphoreType.DMA
    scratch = [
        vm((micro, rows, width), bf),
        vm((micro, rows, width), bf),
        vm((2, width, half // 2), bf),
        vm((2, width, feat), bf),
        vm((micro, rows, feat), bf),
        vm((4, micro, 3, rows, half), bf),
        vm((micro, 2, rows, half), bf),
        vm((micro, rows, half), bf),
        vm((micro, 2, 2, rows, half), bf),
        vm((micro, 2, rows, half), bf),
        vm((micro, 2, feat, rows), bf),
        vm((micro, 2, feat, rows), bf),
        vm((micro, feat, rows), bf),
        vm((micro, feat, rows), bf),
        vm((micro, feat, rows), f32),
        vm((micro, feat, rows), bf),
        vm((micro, feat, rows), bf),
        dma, dma((2,)), dma((2,)), dma((micro,)),
    ]
    scratch += [dma((steps,))] * 8
    scratch += [dma((4 * micro,))] * 2
    scratch += [dma((micro * pairs,))] * 4
    scratch += [dma((2 * micro,))] * 2
    scratch += [dma((steps,))] * 4
    work = 2 * micro * rows * width * feat * 5
    out = pl.pallas_call(
        lambda *refs: relay_kernel(n_segment, *refs),
        out_shape=jax.ShapeDtypeStruct((micro, rows, feat), bf),
        in_specs=[pl.BlockSpec(memory_space=pl.ANY)] * 3,
        out_specs=pl.BlockSpec(memory_space=pltpu.VMEM),
        scratch_shapes=scratch,
        compiler_params=pltpu.CompilerParams(
            collective_id=0, has_side_effects=True, vmem_limit_bytes=62 * 1024 * 1024),
        cost_estimate=pl.CostEstimate(flops=work, bytes_accessed=32 << 20, transcendentals=1 << 23),
        name="relay",
    )(inbound[0], jnp.transpose(weights[0], (1, 0, 2)), cotangent[0])
    return out[None]


def solution(mesh):
    sizes = dict(mesh.shape)
    fused = sizes["dp"] == 2 and sizes["tensor"] == 4

    def run(inbound, weights, cotangent):
        if fused and inbound.shape[1] == 2 and weights.shape[3] % 512 == 0 and inbound.shape[2] % 256 == 0:
            return fused_shards(sizes["segment"], inbound, weights, cotangent)
        return shards(inbound, weights, cotangent)

    placed = (
        P("segment", None, "dp", None),
        P("segment", None, None, "tensor"),
        P("segment", None, "dp", "tensor"),
    )
    return jax.shard_map(
        run,
        mesh=mesh,
        in_specs=placed,
        out_specs=P("segment", None, "dp", "tensor"),
        check_vma=False,
    )
```
